32 devices in a mesh: lon: 8 (over z, x), lat: 4 (over y, core).
Axes of the slice: x: 2, y: 2, z: 4, core: 2. Of those that a mesh axis runs over, the one named last changes fastest.
Arguments:
- adj_elev: float32 [1280, 5120], P('lon', 'lat'), may hold values from -6 to 6
- adj_east: float32 [1280, 5120], P('lon', 'lat'), may hold values from -6 to 6
- adj_north: float32 [1280, 5120], P('lon', 'lat'), may hold values from -6 to 6
- depth: float32 [1280, 5120], P('lon', 'lat'), may hold values from 0.5 to 2
- friction: float32 [1280, 5120], P('lon', 'lat'), may hold values from 0.01 to 0.3
- ocean_mask: int32 [1280, 5120], P('lon', 'lat'), may hold values 0 or 1
- misfit_values: float32 [4, 8192, 256], P(None, ('lon', 'lat')), may hold values from -6 to 6
- dest_lon: int32 [4, 8192, 1], P(None, ('lon', 'lat')), may hold values from 0 to 7; in each aligned block of 256 rows (0 to 255, 256 to 511, ..., all dimensions but the last counted through in order) at most 64 rows name the same one
- block_cell: int32 [4, 8192], P(None, ('lon', 'lat')), may hold values from 0 to 799
Outputs:
- out_elev: float32 [1280, 5120], P('lon', 'lat')
- out_east: float32 [1280, 5120], P('lon', 'lat')
- out_north: float32 [1280, 5120], P('lon', 'lat')
The draws below stay inside these ranges and needn't reach their ends.
Inputs may be any that keep to these rules, and one draw needn't show every extreme that they name: `dest_lon`: in each step, the 256 rows of one pass owner name each longitude tile at most 64 times, and some owner reaches 64. `block_cell`: several blocks may name the same cell block.
All inputs are finite; a program needn't handle non-finite values. No bound on the sum of `ocean_mask` on one device may be relied on, other than what follows from the above.
Results may differ from the reference program's by a relative error of at most 0.00002.
Values sent between devices are 32-bit elements; how exact they have to be, the bound alone decides.
A program may use at most 128 MiB of HBM per device.

```python
import math
import jax
import jax.numpy as jnp
import numpy as np

CLON = 160
CLAT = 1280
B_DEV = 256
STEPS = 4
NLON = 1280
NLAT = 5120
ROWS = 8192
CAP = 64
TILE_BLOCKS = 800
N_LON = 8
N_LAT = 4


def place_ends(values, own_key, smallest, largest):
    spot = [jax.random.randint(jax.random.fold_in(own_key, axis), (), 0, length) for axis, length in enumerate(values.shape)]
    longest = values.shape.index(max(values.shape))
    next_to = spot[:longest] + [(spot[longest] + 1) % values.shape[longest]] + spot[longest + 1:]
    return values.at[tuple(spot)].set(smallest).at[tuple(next_to)].set(largest)


def steps_of(key, extent, split, smallest, top_value):
    level, own = 1.0, jax.random.fold_in(key, 6)
    for axis_at, blocks in split:
        heights = jnp.exp(jax.random.uniform(jax.random.fold_in(own, axis_at), (blocks,), jnp.float32, smallest / len(split), top_value / len(split)))
        level = level * jnp.repeat(heights, extent[axis_at] // blocks).reshape([-1 if axis == axis_at else 1 for axis in range(len(extent))])
    return level


def shared_out(key, own, number, rows, count, top, most, slope):
    ranking = jax.random.permutation(key, count)
    packed, usual = shares(count, rows * top, most, slope, True), shares(count, rows * top, most, slope, False)
    places = jnp.arange(count)

    def named(lengths, offset_by):
        used = int((lengths > 0).sum())
        fixed = max(1, used // 4)
        shifted = fixed + (places - fixed + offset_by * (used - fixed)) % max(1, count - fixed)
        return jnp.zeros((count,), jnp.int32).at[ranking[jnp.where(places < fixed, places, shifted)]].set(jnp.asarray(lengths, jnp.int32))

    lengths = jnp.where(number % 4 == 0, named(packed, number // 4), named(usual, number - number // 4 - 1))
    mixed = jax.random.permutation(jax.random.fold_in(own, 3), count)
    giver, taker = mixed[0:count // 2 * 2:2], mixed[1:count // 2 * 2:2]
    slack = jnp.minimum(lengths[giver] - 1, most - lengths[taker]) // 2
    slack = jnp.where((giver == ranking[0]) | (taker == ranking[0]) | (lengths[taker] == 0), 0, jnp.maximum(slack, 0))
    shifted = jax.random.randint(jax.random.fold_in(own, 4), (count // 2,), 0, 1 << 20) % (slack + 1)
    lengths = lengths.at[giver].add(-shifted).at[taker].add(shifted)
    members = jnp.searchsorted(jnp.cumsum(lengths), jnp.arange(rows * top), side="right").astype(jnp.int32)
    table = members.reshape(top, rows).T
    table = table[jax.random.permutation(jax.random.fold_in(own, 1), rows)]
    offset_by = jax.random.randint(jax.random.fold_in(own, 2), (rows, 1), 0, top)
    return jnp.take_along_axis(table, (jnp.arange(top)[None, :] + offset_by) % top, axis=1)


def shares(number_of, total, most, lean, full):
    portions = [(1 << 20) // math.isqrt(rank ** lean) + 1 for rank in range(1, number_of + 1)]
    largest = most if full else min(most, max(-(-total // number_of), total * portions[0] // sum(portions)))
    least = 1 if total - largest >= number_of - 1 else 0
    counts, surplus = [largest] + [least] * (number_of - 1), total - largest - least * (number_of - 1)
    while surplus > 0:
        free = [i for i in range(1, number_of) if counts[i] < largest] or [i for i in range(1, number_of) if counts[i] < most]
        mass, remaining = sum([portions[i] for i in free]), surplus
        for i in free:
            extra = min(most - counts[i], max(1, remaining * portions[i] // mass), surplus)
            counts[i] = counts[i] + extra
            surplus = surplus - extra
    return np.array(counts)


def scatter_about(stream_key, extent, spread, limit, pieces=(), kind=jnp.bfloat16):
    entries = jax.random.normal(stream_key, extent, jnp.float32) * spread
    if len(pieces) > 0:
        entries = steps_of(stream_key, extent, pieces, -0.22, 0.18) * entries
    return jnp.clip(entries, min=-limit, max=limit).astype(kind)


def setup_inputs(seed: int = 0) -> dict:
    key_of = jax.random.split(jax.random.key(seed), 10)
    adj_elev = scatter_about(key_of[0], (NLON, NLAT), 1.0, 6.0, ((0, 8), (1, 4)), jnp.float32)
    adj_east = scatter_about(key_of[1], (NLON, NLAT), 1.0, 6.0, ((0, 8), (1, 4)), jnp.float32)
    adj_north = scatter_about(key_of[2], (NLON, NLAT), 1.0, 6.0, ((0, 8), (1, 4)), jnp.float32)
    depth = jnp.clip(0.5 + 1.5 * jax.random.uniform(key_of[3], (NLON, NLAT), jnp.float32) ** steps_of(key_of[3], (NLON, NLAT), ((0, 8), (1, 4)), -0.2, 0.2), 0.5, 2.0)
    friction = jnp.clip(jnp.exp(math.log(0.3) - 3.4011974 * jax.random.uniform(key_of[4], (NLON, NLAT), jnp.float32) ** steps_of(key_of[4], (NLON, NLAT), ((0, 8), (1, 4)), -0.2, 0.2)), 0.01, 0.3)
    ocean_mask = place_ends((jax.random.randint(key_of[5], (NLON, NLAT), 0, 10) < 7).astype(jnp.int32), jax.random.fold_in(key_of[5], 1), 0, 1)
    misfit_values = scatter_about(key_of[6], (STEPS, ROWS, 256), 1.0, 6.0, ((1, 32),), jnp.float32)
    dest_lon_keys = jax.random.split(jax.random.fold_in(key_of[7], 1), STEPS * ROWS // B_DEV)
    dest_lon_turns = jax.random.permutation(jax.random.fold_in(key_of[7], 3), STEPS * ROWS // B_DEV)
    dest_lon = jax.vmap(lambda own, number: shared_out(jax.random.fold_in(key_of[7], 2), own, number, B_DEV, N_LON, 1, CAP, 2))(dest_lon_keys, dest_lon_turns).reshape((STEPS, ROWS, 1))
    block_cell = place_ends(jax.random.randint(key_of[8], (STEPS, ROWS), 0, TILE_BLOCKS), jax.random.fold_in(key_of[8], 1), 0, TILE_BLOCKS - 1).astype(jnp.int32)
    return dict(adj_elev=adj_elev, adj_east=adj_east, adj_north=adj_north, depth=depth, friction=friction, ocean_mask=ocean_mask, misfit_values=misfit_values, dest_lon=dest_lon, block_cell=block_cell)


def grid_forcing(values, dest, cells):
    rows = values.shape[0]
    per_lat = CLAT // 16
    per_lon = CLON // 16
    owner_lat = (jnp.arange(rows, dtype=jnp.int32) // B_DEV) % N_LAT
    lon_block = dest[:, 0] * per_lon + cells // per_lat
    lat_block = owner_lat * per_lat + cells % per_lat
    flat = lon_block * (NLAT // 16) + lat_block
    blocks = jnp.zeros(((NLON // 16) * (NLAT // 16), 256), jnp.float32).at[flat].add(values)
    blocks = blocks.reshape(NLON // 16, NLAT // 16, 16, 16).transpose(0, 2, 1, 3)
    return blocks.reshape(NLON, NLAT)


def reference(adj_elev, adj_east, adj_north, depth, friction, ocean_mask, misfit_values, dest_lon, block_cell):
    wet = ocean_mask.astype(jnp.float32)
    wall = (jnp.arange(NLAT) < NLAT - 1).astype(jnp.float32)[None, :]
    elev, east, north = adj_elev, adj_east, adj_north
    zero_col = jnp.zeros((NLON, 1), jnp.float32)
    for step in reversed(range(STEPS)):
        elev = elev + wet * grid_forcing(misfit_values[step], dest_lon[step], block_cell[step])
        elev_east = jnp.roll(elev, -1, axis=0)
        elev_north = jnp.concatenate([elev[:, 1:], zero_col], axis=1)
        flow_u = wet * (east + 0.25 * (elev_east - elev))
        flow_v = wet * wall * (north + 0.25 * (elev_north - elev))
        term_u = depth * flow_u
        term_v = depth * flow_v
        term_west = jnp.roll(term_u, 1, axis=0)
        term_south = jnp.concatenate([zero_col, term_v[:, :-1]], axis=1)
        elev = elev + 0.25 * (term_u - term_west) + 0.25 * (term_v - term_south)
        east = (1.0 - friction) * flow_u
        north = (1.0 - friction) * flow_v
    return elev, east, north
```

```python
import jax
import jax.numpy as jnp
from jax import lax
from jax.sharding import PartitionSpec as P


def passed_along(x, axis, by):
    size = lax.axis_size(axis)
    return lax.ppermute(x, axis, [(i, (i + by) % size) for i in range(size)])


def from_behind(block, axis, distance):
    devices = range(lax.axis_size(axis))
    route = [(i - distance, i) for i in devices if i - distance in devices]
    return lax.ppermute(block, axis, route)


def bucket_blocks(values, dest, cells, n_lon, slots):
    target = dest[:, 0]
    rank = jnp.arange(target.shape[0], dtype=jnp.int32)
    earlier = (target[:, None] == target[None, :]) & (rank[None, :] < rank[:, None])
    place = jnp.sum(earlier.astype(jnp.int32), axis=1)
    flat = target * slots + place
    value_buf = jnp.zeros((n_lon * slots, 256), jnp.float32).at[flat].set(values)
    index_buf = jnp.zeros((n_lon * slots,), jnp.int32).at[flat].set(cells)
    return (value_buf.reshape(n_lon, slots, 256), index_buf.reshape(n_lon, slots))


def tile_forcing(values, indices, tile_lon, tile_lat):
    count = tile_lon // 16 * (tile_lat // 16)
    blocks = (
        jnp.zeros((count, 256), jnp.float32).at[indices.reshape(-1)].add(values.reshape(-1, 256))
    )
    blocks = blocks.reshape(tile_lon // 16, tile_lat // 16, 16, 16).transpose(0, 2, 1, 3)
    return blocks.reshape(tile_lon, tile_lat)


def adjoint_step(elev, east, north, depth, friction, wet, wall):
    head = passed_along(elev[0:1, :], "lon", -1)
    elev_east = jnp.concatenate([elev[1:, :], head], axis=0)
    side = from_behind(elev[:, 0:1], "lat", -1)
    elev_north = jnp.concatenate([elev[:, 1:], side], axis=1)
    flow_u = wet * (east + 0.25 * (elev_east - elev))
    flow_v = wet * wall * (north + 0.25 * (elev_north - elev))
    term_u = depth * flow_u
    term_v = depth * flow_v
    tail = passed_along(term_u[-1:, :], "lon", 1)
    term_west = jnp.concatenate([tail, term_u[:-1, :]], axis=0)
    lower = from_behind(term_v[:, -1:], "lat", 1)
    term_south = jnp.concatenate([lower, term_v[:, :-1]], axis=1)
    elev = elev + 0.25 * (term_u - term_west) + 0.25 * (term_v - term_south)
    return (elev, (1.0 - friction) * flow_u, (1.0 - friction) * flow_v)


def per_device(
    adj_elev, adj_east, adj_north, depth, friction, ocean_mask, misfit_values, dest_lon, block_cell
):
    tile_lon, tile_lat = adj_elev.shape
    n_lon = lax.axis_size("lon")
    n_steps, owned, width = misfit_values.shape
    slots = 2 * owned // n_lon
    wet = ocean_mask.astype(jnp.float32)
    packed = [
        bucket_blocks(misfit_values[step], dest_lon[step], block_cell[step], n_lon, slots)
        for step in range(n_steps)
    ]
    forcings = []
    for step in range(n_steps):
        got_values, got_indices = (
            lax.all_to_all(packed[step][0], "lon", split_axis=0, concat_axis=0, tiled=True),
            lax.all_to_all(packed[step][1], "lon", split_axis=0, concat_axis=0, tiled=True),
        )
        forcings.append(tile_forcing(got_values, got_indices, tile_lon, tile_lat))
    total_lat = tile_lat * lax.axis_size("lat")
    global_lat = lax.axis_index("lat") * tile_lat + jnp.arange(tile_lat, dtype=jnp.int32)
    wall = (global_lat < total_lat - 1).astype(jnp.float32)[None, :]
    elev, east, north = (adj_elev, adj_east, adj_north)
    for step in reversed(range(n_steps)):
        elev = elev + wet * forcings[step]
        elev, east, north = adjoint_step(elev, east, north, depth, friction, wet, wall)
    return (elev, east, north)


def solution(mesh):
    placed = (
        P("lon", "lat"),
        P("lon", "lat"),
        P("lon", "lat"),
        P("lon", "lat"),
        P("lon", "lat"),
        P("lon", "lat"),
        P(None, ("lon", "lat"), None),
        P(None, ("lon", "lat"), None),
        P(None, ("lon", "lat")),
    )
    return jax.shard_map(
        per_device,
        mesh=mesh,
        in_specs=placed,
        out_specs=(P("lon", "lat"), P("lon", "lat"), P("lon", "lat")),
        check_vma=False,
    )
```

```python
import functools

import jax
import jax.numpy as jnp
from jax import lax
from jax.experimental import pallas as pl
from jax.experimental.pallas import tpu as pltpu
from jax.sharding import PartitionSpec as P

F32, BF16 = jnp.float32, jnp.bfloat16
MESH = pl.DeviceIdType.MESH
SIDE = 16
NT = (((1,), (1,)), ((), ()))


def split(x):
    high = x.astype(BF16)
    return high, (x - high.astype(F32)).astype(BF16)


def iota(shape, dim):
    return lax.broadcasted_iota(jnp.int32, shape, dim)


def hot(condition):
    return jnp.where(condition, 1.0, 0.0).astype(BF16)


def kernel(
    n_lon, n_lat,
    values, meta, elev_in, east_in, north_in, depth_in, friction_in, mask_in,
    out_e, out_u, out_v,
    send, recv, cell_send, cell_recv, cells, spread, turned, mixed,
    elev, depth, friction, mask, col_n, col_s,
    to_w, to_e, to_s, to_n, from_e, from_w, from_n, from_s,
    load_sem, send_sem, recv_sem, cell_sems, halo_send, halo_recv,
):
    steps, owned, width = values.shape
    rows, cols = out_e.shape
    slots = 2 * owned // n_lon
    total = n_lon * slots
    per_lane = 128 // slots
    n_bi, n_bj = rows // SIDE, cols // SIDE
    wide = to_s.shape[-1]
    lon, lat = lax.axis_index("lon"), lax.axis_index("lat")

    loads = [
        pltpu.make_async_copy(src, dst, load_sem.at[i])
        for i, (src, dst) in enumerate((
            (elev_in, elev.at[pl.ds(0, rows), :]), (east_in, out_u), (north_in, out_v),
            (depth_in, depth), (friction_in, friction), (mask_in, mask),
        ))
    ]
    for load in loads:
        load.start()

    barrier = pltpu.get_barrier_semaphore()

    def peer(k):
        return lax.rem(lon + k, n_lon)

    @pl.loop(1, n_lon)
    def _(k):
        pl.semaphore_signal(barrier, inc=1, device_id={"lon": peer(k)}, device_id_type=MESH)

    north_of, south_of = lax.rem(lat + 1, n_lat), lax.rem(lat + n_lat - 1, n_lat)
    for there in (north_of, south_of):
        pl.semaphore_signal(barrier, inc=1, device_id={"lat": there}, device_id_type=MESH)

    lower = hot(iota((owned, owned), 0) < iota((owned, owned), 1))
    shift = lax.rem(lon * slots, 128)

    def placed(s):
        dest = meta[s][0:1, :]
        picked = hot(iota((n_lon, owned), 0) == dest)
        before = jnp.dot(picked, lower, preferred_element_type=F32)
        place = jnp.sum(before * picked.astype(F32), axis=0, keepdims=True)
        return dest, place.astype(jnp.int32)

    bundle = jnp.zeros((n_lon * 8, 128), F32)
    for s in range(steps):
        dest, place = placed(s)
        at = iota((8, owned), 0)
        info = meta[s].astype(F32)
        line = jnp.where(at == s, info[1:2, :], jnp.where(at == steps + s, info[2:3, :], 0.0))
        line = jnp.concatenate([line] * n_lon, axis=0)
        line = jnp.where((iota((n_lon * 8, owned), 0) >> 3) == dest, line, 0.0).astype(BF16)
        lane = hot(iota((128, owned), 0) == place + shift)
        bundle = bundle + lax.dot_general(line, lane, NT, preferred_element_type=F32)
    cell_send[...] = bundle.reshape(n_lon, 8, 128)

    pl.semaphore_wait(barrier, n_lon + 1)

    @pl.loop(1, n_lon)
    def _(k):
        pltpu.make_async_remote_copy(
            src_ref=cell_send.at[peer(k)], dst_ref=cell_recv.at[lon],
            send_sem=cell_sems.at[0], recv_sem=cell_sems.at[1],
            device_id={"lon": peer(k)}, device_id_type=MESH,
        ).start()

    @pl.loop(0, steps)
    def _(i):
        s = steps - 1 - i
        dest, place = placed(s)
        pick = hot(iota((total, owned), 0) == dest * slots + place)
        high, low = split(values[s])
        send[s] = jnp.dot(pick, high, preferred_element_type=F32) + jnp.dot(
            pick, low, preferred_element_type=F32
        )

        @pl.loop(1, n_lon)
        def _(k):
            pltpu.make_async_remote_copy(
                src_ref=send.at[s, pl.ds(peer(k) * slots, slots), :],
                dst_ref=recv.at[s, pl.ds(lon * slots, slots), :],
                send_sem=send_sem.at[s], recv_sem=recv_sem.at[s],
                device_id={"lon": peer(k)}, device_id_type=MESH,
            ).start()

        mine = pl.ds(pl.multiple_of(lon * slots, 8), slots)
        recv[s, mine, :] = send[s, mine, :]

    cell_recv[lon] = cell_send[lon]

    for b in range(SIDE):
        spread[b * 128:(b + 1) * 128, :] = hot(iota((128, cols), 1) == iota((128, cols), 0) * SIDE + b)
    at = iota((width, width), 0)
    turn = hot(iota((width, width), 1) == (at % SIDE) * SIDE + at // SIDE)
    eye = iota((rows, wide), 0) == iota((rows, wide), 1)

    def laid(column):
        return jnp.sum(jnp.where(eye, column, 0.0), axis=0, keepdims=True)

    def stood(line):
        return jnp.sum(jnp.where(eye, line, 0.0), axis=1, keepdims=True)

    for load in loads:
        load.wait()

    others = pl.ds(0, n_lon - 1)
    pltpu.make_async_copy(cell_recv.at[others], cell_recv.at[others], cell_sems.at[1]).wait()
    for g in range(total // 128):
        part = cell_recv[g * per_lane:(g + 1) * per_lane]
        cells[:, g * 128:(g + 1) * 128] = jnp.sum(part, axis=0)

    last = jnp.where(lat == n_lat - 1, 1, 0)
    open_lat = jnp.where(lat == 0, 0.0, 1.0)
    most = pl.ds(0, (n_lon - 1) * slots)
    end = cols - 128

    @pl.loop(0, steps)
    def _(i):
        s = steps - 1 - i
        pltpu.make_async_copy(recv.at[s, most, :], recv.at[s, most, :], recv_sem.at[s]).wait()
        bi = cells[pl.ds(s, 1), :].astype(jnp.int32)
        bj = cells[pl.ds(steps + s, 1), :].astype(jnp.int32)
        for h, part in enumerate(split(recv[s])):
            turned[h] = lax.dot_general(turn, part, NT, preferred_element_type=F32).astype(BF16)
        keep = hot((iota((rows, total), 0) // SIDE) == bi)
        column = hot(iota((128, total), 0) == bj)
        for b in range(SIDE):
            both = jnp.concatenate(
                [jnp.concatenate([turned[h, b * SIDE:(b + 1) * SIDE, :]] * n_bi, axis=0) * keep for h in range(2)],
                axis=0,
            )
            got = lax.dot_general(both, column, NT, preferred_element_type=F32)
            high, low = split(got[:rows] + got[rows:])
            mixed[:rows, b * 128:(b + 1) * 128] = high
            mixed[rows:, b * 128:(b + 1) * 128] = low
        for n in range(cols // 256):
            here = slice(n * 256, (n + 1) * 256)
            force = jnp.dot(mixed[...], spread[:, here], preferred_element_type=F32)
            elev[:rows, here] = elev[:rows, here] + mask[:, here].astype(F32) * (force[:rows] + force[rows:])

        to_w[s] = elev[0:1, :]
        to_e[s, :, 0:cols] = elev[rows - 1:rows, :]
        to_e[s, :, cols:2 * cols] = out_u[rows - 1:rows, :]
        to_e[s, :, 2 * cols:] = depth[rows - 1:rows, :] * mask[rows - 1:rows, :].astype(F32)
        first = laid(elev[:rows, 0:128][:, 0:1])
        to_s[s] = first
        to_n[s, :, 0:wide] = laid(elev[:rows, end:][:, 127:128])
        to_n[s, :, wide:2 * wide] = laid(out_v[:, end:][:, 127:128])
        to_n[s, :, 2 * wide:] = laid((depth[:, end:] * mask[:, end:].astype(F32))[:, 127:128])
        copies = [
            pltpu.make_async_remote_copy(
                src_ref=src.at[s], dst_ref=dst.at[s],
                send_sem=halo_send.at[s, q], recv_sem=halo_recv.at[s, q],
                device_id=there, device_id_type=MESH,
            )
            for q, (src, dst, there) in enumerate((
                (to_w, from_e, {"lon": peer(n_lon - 1)}),
                (to_e, from_w, {"lon": peer(1)}),
                (to_s, from_n, {"lat": south_of}),
                (to_n, from_s, {"lat": north_of}),
            ))
        ]
        for copy in copies:
            copy.start()
        for copy in copies:
            copy.wait()
        elev[rows:rows + 1, :] = from_e[s]
        col_n[...] = stood(from_n[s])
        side = from_s[s]
        col_s[...] = stood(
            open_lat * side[:, 2 * wide:]
            * (side[:, wide:2 * wide] + 0.25 * (first - side[:, 0:wide]))
        )
        edge = from_w[s]
        above = edge[:, 2 * cols:] * (
            edge[:, cols:2 * cols] + 0.25 * (elev[0:1, :] - edge[:, 0:cols])
        )
        row_at, lane_at = iota((8, cols), 0), iota((8, cols), 1)

        def chunk(k, above):
            here = pl.ds(pl.multiple_of(k * 8, 8), 8)
            e = elev[here, :]
            e_next = elev[pl.ds(pl.multiple_of(k * 8 + 8, 8), 8), :]
            wet = mask[here, :].astype(F32)
            wet_v = jnp.where(lane_at < cols - last, wet, 0.0)
            e_east = jnp.where(row_at == 7, e_next[0:1, :], pltpu.roll(e, 7, 0))
            e_north = jnp.where(lane_at == cols - 1, col_n[here, :], pltpu.roll(e, cols - 1, 1))
            flow_u = wet * (out_u[here, :] + 0.25 * (e_east - e))
            flow_v = wet_v * (out_v[here, :] + 0.25 * (e_north - e))
            deep = depth[here, :]
            term_u, term_v = deep * flow_u, deep * flow_v
            west = jnp.where(row_at == 0, above, pltpu.roll(term_u, 1, 0))
            south = jnp.where(lane_at == 0, col_s[here, :], pltpu.roll(term_v, 1, 1))
            e = e + 0.25 * (term_u - west) + 0.25 * (term_v - south)
            elev[here, :] = e
            out_e[here, :] = e
            slow = 1.0 - friction[here, :]
            out_u[here, :] = slow * flow_u
            out_v[here, :] = slow * flow_v
            return term_u[7:8, :]

        lax.fori_loop(0, rows // 8, chunk, above)

    pltpu.make_async_copy(cell_send.at[others], cell_send.at[others], cell_sems.at[0]).wait()

    @pl.loop(0, steps)
    def _(s):
        pltpu.make_async_copy(send.at[s, most, :], send.at[s, most, :], send_sem.at[s]).wait()


def per_device(
    n_lon, n_lat,
    adj_elev, adj_east, adj_north, depth, friction, ocean_mask, misfit_values, dest_lon, block_cell,
):
    rows, cols = adj_elev.shape
    steps, owned, width = misfit_values.shape
    slots = 2 * owned // n_lon
    total = n_lon * slots
    per_lat = cols // SIDE
    meta = jnp.stack([dest_lon[:, :, 0], block_cell // per_lat, block_cell % per_lat], axis=1)
    meta = jnp.pad(meta, ((0, 0), (0, 5), (0, 0)))
    wide = -(-rows // 128) * 128
    vmem = pl.BlockSpec(memory_space=pltpu.VMEM)
    hbm = pl.BlockSpec(memory_space=pl.ANY)
    tile = jax.ShapeDtypeStruct((rows, cols), F32)
    return pl.pallas_call(
        functools.partial(kernel, n_lon, n_lat),
        out_shape=(tile, tile, tile),
        in_specs=[vmem] * 2 + [hbm] * 6,
        out_specs=(vmem, vmem, vmem),
        scratch_shapes=[
            pltpu.VMEM((steps, total, width), F32),
            pltpu.VMEM((steps, total, width), F32),
            pltpu.VMEM((n_lon, 8, 128), F32),
            pltpu.VMEM((n_lon, 8, 128), F32),
            pltpu.VMEM((8, total), F32),
            pltpu.VMEM((SIDE * 128, cols), BF16),
            pltpu.VMEM((2, width, total), BF16),
            pltpu.VMEM((2 * rows, SIDE * 128), BF16),
            pltpu.VMEM((rows + 8, cols), F32),
            pltpu.VMEM((rows, cols), F32),
            pltpu.VMEM((rows, cols), F32),
            pltpu.VMEM((rows, cols), jnp.int32),
            pltpu.VMEM((rows, 1), F32),
            pltpu.VMEM((rows, 1), F32),
            pltpu.VMEM((steps, 1, cols), F32),
            pltpu.VMEM((steps, 1, 3 * cols), F32),
            pltpu.VMEM((steps, 1, wide), F32),
            pltpu.VMEM((steps, 1, 3 * wide), F32),
            pltpu.VMEM((steps, 1, cols), F32),
            pltpu.VMEM((steps, 1, 3 * cols), F32),
            pltpu.VMEM((steps, 1, wide), F32),
            pltpu.VMEM((steps, 1, 3 * wide), F32),
            pltpu.SemaphoreType.DMA((6,)),
            pltpu.SemaphoreType.DMA((steps,)),
            pltpu.SemaphoreType.DMA((steps,)),
            pltpu.SemaphoreType.DMA((2,)),
            pltpu.SemaphoreType.DMA((steps, 4)),
            pltpu.SemaphoreType.DMA((steps, 4)),
        ],
        compiler_params=pltpu.CompilerParams(
            collective_id=0, has_side_effects=True, vmem_limit_bytes=48 * 2**20
        ),
    )(misfit_values, meta, adj_elev, adj_east, adj_north, depth, friction, ocean_mask)


def solution(mesh):
    tile, owned = P("lon", "lat"), P(None, ("lon", "lat"))
    return jax.shard_map(
        functools.partial(per_device, mesh.shape["lon"], mesh.shape["lat"]),
        mesh=mesh,
        in_specs=(tile,) * 6 + (P(None, ("lon", "lat"), None), P(None, ("lon", "lat"), None), owned),
        out_specs=(tile, tile, tile),
        check_vma=False,
    )
```

```python
import functools

import jax
import jax.numpy as jnp
from jax import lax
from jax.experimental import pallas as pl
from jax.experimental.pallas import tpu as pltpu
from jax.sharding import PartitionSpec as P

F32, BF16 = jnp.float32, jnp.bfloat16
MESH = pl.DeviceIdType.MESH
SIDE = 16
NT = (((1,), (1,)), ((), ()))


def split(x):
    high = x.astype(BF16)
    return high, (x - high.astype(F32)).astype(BF16)


def iota(shape, dim):
    return lax.broadcasted_iota(jnp.int32, shape, dim)


def hot(condition):
    return jnp.where(condition, 1.0, 0.0).astype(BF16)


def kernel(
    n_lon, n_lat,
    values, meta, elev_in, east_in, north_in, depth_in, friction_in, mask_in,
    out_e, out_u, out_v,
    send, recv, cell_send, cell_recv, cells, spread, turned, mixed, force,
    elev, depth, friction, mask, col_n, col_s,
    to_w, to_e, to_s, to_n, from_e, from_w, from_n, from_s,
    load_sem, send_sem, recv_sem, cell_sems, halo_send, halo_recv,
):
    steps, owned, width = values.shape
    rows, cols = out_e.shape
    slots = 2 * owned // n_lon
    total = n_lon * slots
    per_lane = 128 // slots
    n_bi, n_bj = rows // SIDE, cols // SIDE
    wide = to_s.shape[-1]
    lon, lat = lax.axis_index("lon"), lax.axis_index("lat")

    loads = [
        pltpu.make_async_copy(src, dst, load_sem.at[i])
        for i, (src, dst) in enumerate((
            (elev_in, elev.at[pl.ds(0, rows), :]), (east_in, out_u), (north_in, out_v),
            (depth_in, depth), (friction_in, friction), (mask_in, mask),
        ))
    ]
    for load in loads:
        load.start()

    barrier = pltpu.get_barrier_semaphore()

    def peer(k):
        return lax.rem(lon + k, n_lon)

    @pl.loop(1, n_lon)
    def _(k):
        pl.semaphore_signal(barrier, inc=1, device_id={"lon": peer(k)}, device_id_type=MESH)

    north_of, south_of = lax.rem(lat + 1, n_lat), lax.rem(lat + n_lat - 1, n_lat)
    for there in (north_of, south_of):
        pl.semaphore_signal(barrier, inc=1, device_id={"lat": there}, device_id_type=MESH)

    lower = hot(iota((owned, owned), 0) < iota((owned, owned), 1))
    shift = lax.rem(lon * slots, 128)

    def placed(s):
        dest = meta[s][0:1, :]
        picked = hot(iota((n_lon, owned), 0) == dest)
        before = jnp.dot(picked, lower, preferred_element_type=F32)
        place = jnp.sum(before * picked.astype(F32), axis=0, keepdims=True)
        return dest, place.astype(jnp.int32)

    bundle = jnp.zeros((n_lon * 8, 128), F32)
    for s in range(steps):
        dest, place = placed(s)
        at = iota((8, owned), 0)
        info = meta[s].astype(F32)
        line = jnp.where(at == s, info[1:2, :], jnp.where(at == steps + s, info[2:3, :], 0.0))
        line = jnp.concatenate([line] * n_lon, axis=0)
        line = jnp.where((iota((n_lon * 8, owned), 0) >> 3) == dest, line, 0.0).astype(BF16)
        lane = hot(iota((128, owned), 0) == place + shift)
        bundle = bundle + lax.dot_general(line, lane, NT, preferred_element_type=F32)
    cell_send[...] = bundle.reshape(n_lon, 8, 128)

    pl.semaphore_wait(barrier, n_lon + 1)

    @pl.loop(1, n_lon)
    def _(k):
        pltpu.make_async_remote_copy(
            src_ref=cell_send.at[peer(k)], dst_ref=cell_recv.at[lon],
            send_sem=cell_sems.at[0], recv_sem=cell_sems.at[1],
            device_id={"lon": peer(k)}, device_id_type=MESH,
        ).start()

    @pl.loop(0, steps)
    def _(i):
        s = steps - 1 - i
        dest, place = placed(s)
        pick = hot(iota((total, owned), 0) == dest * slots + place)
        high, low = split(values[s])
        send[s] = jnp.dot(pick, high, preferred_element_type=F32) + jnp.dot(
            pick, low, preferred_element_type=F32
        )

        @pl.loop(1, n_lon)
        def _(k):
            pltpu.make_async_remote_copy(
                src_ref=send.at[s, pl.ds(peer(k) * slots, slots), :],
                dst_ref=recv.at[s, pl.ds(lon * slots, slots), :],
                send_sem=send_sem.at[s], recv_sem=recv_sem.at[s],
                device_id={"lon": peer(k)}, device_id_type=MESH,
            ).start()

        mine = pl.ds(pl.multiple_of(lon * slots, 8), slots)
        recv[s, mine, :] = send[s, mine, :]

    cell_recv[lon] = cell_send[lon]

    for b in range(SIDE):
        spread[b * 128:(b + 1) * 128, :] = hot(iota((128, cols), 1) == iota((128, cols), 0) * SIDE + b)
    at = iota((width, width), 0)
    turn = hot(iota((width, width), 1) == (at % SIDE) * SIDE + at // SIDE)
    eye = iota((rows, wide), 0) == iota((rows, wide), 1)

    def laid(column):
        return jnp.sum(jnp.where(eye, column, 0.0), axis=0, keepdims=True)

    def stood(line):
        return jnp.sum(jnp.where(eye, line, 0.0), axis=1, keepdims=True)

    for load in loads:
        load.wait()

    others = pl.ds(0, n_lon - 1)
    pltpu.make_async_copy(cell_recv.at[others], cell_recv.at[others], cell_sems.at[1]).wait()
    for g in range(total // 128):
        part = cell_recv[g * per_lane:(g + 1) * per_lane]
        cells[:, g * 128:(g + 1) * 128] = jnp.sum(part, axis=0)

    last = jnp.where(lat == n_lat - 1, 1, 0)
    open_lat = jnp.where(lat == 0, 0.0, 1.0)
    most = pl.ds(0, (n_lon - 1) * slots)
    end = cols - 128

    def scatter(s):
        pltpu.make_async_copy(recv.at[s, most, :], recv.at[s, most, :], recv_sem.at[s]).wait()
        bi = cells[pl.ds(s, 1), :].astype(jnp.int32)
        bj = cells[pl.ds(steps + s, 1), :].astype(jnp.int32)
        for h, part in enumerate(split(recv[s])):
            turned[h] = lax.dot_general(turn, part, NT, preferred_element_type=F32).astype(BF16)
        keep = hot((iota((rows, total), 0) // SIDE) == bi)
        column = hot(iota((128, total), 0) == bj)
        for b in range(SIDE):
            both = jnp.concatenate(
                [jnp.concatenate([turned[h, b * SIDE:(b + 1) * SIDE, :]] * n_bi, axis=0) * keep for h in range(2)],
                axis=0,
            )
            got = lax.dot_general(both, column, NT, preferred_element_type=F32)
            high, low = split(got[:rows] + got[rows:])
            mixed[:rows, b * 128:(b + 1) * 128] = high
            mixed[rows:, b * 128:(b + 1) * 128] = low
        for n in range(cols // 256):
            here = slice(n * 256, (n + 1) * 256)
            got = jnp.dot(mixed[...], spread[:, here], preferred_element_type=F32)
            force[s, :, here] = mask[:, here].astype(F32) * (got[:rows] + got[rows:])

    scatter(steps - 1)

    @pl.loop(0, steps)
    def _(i):
        s = steps - 1 - i
        elev[:rows, :] = elev[:rows, :] + force[s]
        to_w[s] = elev[0:1, :]
        to_e[s, :, 0:cols] = elev[rows - 1:rows, :]
        to_e[s, :, cols:2 * cols] = out_u[rows - 1:rows, :]
        to_e[s, :, 2 * cols:] = depth[rows - 1:rows, :] * mask[rows - 1:rows, :].astype(F32)
        first = laid(elev[:rows, 0:128][:, 0:1])
        to_s[s] = first
        to_n[s, :, 0:wide] = laid(elev[:rows, end:][:, 127:128])
        to_n[s, :, wide:2 * wide] = laid(out_v[:, end:][:, 127:128])
        to_n[s, :, 2 * wide:] = laid((depth[:, end:] * mask[:, end:].astype(F32))[:, 127:128])
        copies = [
            pltpu.make_async_remote_copy(
                src_ref=src.at[s], dst_ref=dst.at[s],
                send_sem=halo_send.at[s, q], recv_sem=halo_recv.at[s, q],
                device_id=there, device_id_type=MESH,
            )
            for q, (src, dst, there) in enumerate((
                (to_w, from_e, {"lon": peer(n_lon - 1)}),
                (to_e, from_w, {"lon": peer(1)}),
                (to_s, from_n, {"lat": south_of}),
                (to_n, from_s, {"lat": north_of}),
            ))
        ]
        for copy in copies:
            copy.start()

        @pl.when(i < steps - 1)
        def _():
            scatter(s - 1)

        for copy in copies:
            copy.wait()
        elev[rows:rows + 1, :] = from_e[s]
        col_n[...] = stood(from_n[s])
        side = from_s[s]
        col_s[...] = stood(
            open_lat * side[:, 2 * wide:]
            * (side[:, wide:2 * wide] + 0.25 * (first - side[:, 0:wide]))
        )
        edge = from_w[s]
        above = edge[:, 2 * cols:] * (
            edge[:, cols:2 * cols] + 0.25 * (elev[0:1, :] - edge[:, 0:cols])
        )
        row_at, lane_at = iota((8, cols), 0), iota((8, cols), 1)

        def chunk(k, above):
            here = pl.ds(pl.multiple_of(k * 8, 8), 8)
            e = elev[here, :]
            e_next = elev[pl.ds(pl.multiple_of(k * 8 + 8, 8), 8), :]
            wet = mask[here, :].astype(F32)
            wet_v = jnp.where(lane_at < cols - last, wet, 0.0)
            e_east = jnp.where(row_at == 7, e_next[0:1, :], pltpu.roll(e, 7, 0))
            e_north = jnp.where(lane_at == cols - 1, col_n[here, :], pltpu.roll(e, cols - 1, 1))
            flow_u = wet * (out_u[here, :] + 0.25 * (e_east - e))
            flow_v = wet_v * (out_v[here, :] + 0.25 * (e_north - e))
            deep = depth[here, :]
            term_u, term_v = deep * flow_u, deep * flow_v
            west = jnp.where(row_at == 0, above, pltpu.roll(term_u, 1, 0))
            south = jnp.where(lane_at == 0, col_s[here, :], pltpu.roll(term_v, 1, 1))
            e = e + 0.25 * (term_u - west) + 0.25 * (term_v - south)
            elev[here, :] = e
            out_e[here, :] = e
            slow = 1.0 - friction[here, :]
            out_u[here, :] = slow * flow_u
            out_v[here, :] = slow * flow_v
            return term_u[7:8, :]

        lax.fori_loop(0, rows // 8, chunk, above)

    pltpu.make_async_copy(cell_send.at[others], cell_send.at[others], cell_sems.at[0]).wait()

    @pl.loop(0, steps)
    def _(s):
        pltpu.make_async_copy(send.at[s, most, :], send.at[s, most, :], send_sem.at[s]).wait()


def per_device(
    n_lon, n_lat,
    adj_elev, adj_east, adj_north, depth, friction, ocean_mask, misfit_values, dest_lon, block_cell,
):
    rows, cols = adj_elev.shape
    steps, owned, width = misfit_values.shape
    slots = 2 * owned // n_lon
    total = n_lon * slots
    per_lat = cols // SIDE
    meta = jnp.stack([dest_lon[:, :, 0], block_cell // per_lat, block_cell % per_lat], axis=1)
    meta = jnp.pad(meta, ((0, 0), (0, 5), (0, 0)))
    wide = -(-rows // 128) * 128
    vmem = pl.BlockSpec(memory_space=pltpu.VMEM)
    hbm = pl.BlockSpec(memory_space=pl.ANY)
    tile = jax.ShapeDtypeStruct((rows, cols), F32)
    return pl.pallas_call(
        functools.partial(kernel, n_lon, n_lat),
        out_shape=(tile, tile, tile),
        in_specs=[vmem] * 2 + [hbm] * 6,
        out_specs=(vmem, vmem, vmem),
        scratch_shapes=[
            pltpu.VMEM((steps, total, width), F32),
            pltpu.VMEM((steps, total, width), F32),
            pltpu.VMEM((n_lon, 8, 128), F32),
            pltpu.VMEM((n_lon, 8, 128), F32),
            pltpu.VMEM((8, total), F32),
            pltpu.VMEM((SIDE * 128, cols), BF16),
            pltpu.VMEM((2, width, total), BF16),
            pltpu.VMEM((2 * rows, SIDE * 128), BF16),
            pltpu.VMEM((steps, rows, cols), F32),
            pltpu.VMEM((rows + 8, cols), F32),
            pltpu.VMEM((rows, cols), F32),
            pltpu.VMEM((rows, cols), F32),
            pltpu.VMEM((rows, cols), jnp.int32),
            pltpu.VMEM((rows, 1), F32),
            pltpu.VMEM((rows, 1), F32),
            pltpu.VMEM((steps, 1, cols), F32),
            pltpu.VMEM((steps, 1, 3 * cols), F32),
            pltpu.VMEM((steps, 1, wide), F32),
            pltpu.VMEM((steps, 1, 3 * wide), F32),
            pltpu.VMEM((steps, 1, cols), F32),
            pltpu.VMEM((steps, 1, 3 * cols), F32),
            pltpu.VMEM((steps, 1, wide), F32),
            pltpu.VMEM((steps, 1, 3 * wide), F32),
            pltpu.SemaphoreType.DMA((6,)),
            pltpu.SemaphoreType.DMA((steps,)),
            pltpu.SemaphoreType.DMA((steps,)),
            pltpu.SemaphoreType.DMA((2,)),
            pltpu.SemaphoreType.DMA((steps, 4)),
            pltpu.SemaphoreType.DMA((steps, 4)),
        ],
        compiler_params=pltpu.CompilerParams(
            collective_id=0, has_side_effects=True, vmem_limit_bytes=60 * 2**20
        ),
    )(misfit_values, meta, adj_elev, adj_east, adj_north, depth, friction, ocean_mask)


def solution(mesh):
    tile, owned = P("lon", "lat"), P(None, ("lon", "lat"))
    return jax.shard_map(
        functools.partial(per_device, mesh.shape["lon"], mesh.shape["lat"]),
        mesh=mesh,
        in_specs=(tile,) * 6 + (P(None, ("lon", "lat"), None), P(None, ("lon", "lat"), None), owned),
        out_specs=(tile, tile, tile),
        check_vma=False,
    )
```

```python
import functools

import jax
import jax.numpy as jnp
from jax import lax
from jax.experimental import pallas as pl
from jax.experimental.pallas import tpu as pltpu
from jax.sharding import PartitionSpec as P

F32, BF16 = jnp.float32, jnp.bfloat16
MESH = pl.DeviceIdType.MESH
SIDE = 16
NT = (((1,), (1,)), ((), ()))


def split(x):
    high = x.astype(BF16)
    return high, (x - high.astype(F32)).astype(BF16)


def iota(shape, dim):
    return lax.broadcasted_iota(jnp.int32, shape, dim)


def hot(condition):
    return jnp.where(condition, 1.0, 0.0).astype(BF16)


def kernel(
    n_lon, n_lat,
    values, meta, elev_in, east_in, north_in, depth_in, friction_in, mask_in,
    out_e, out_u, out_v,
    send, recv, cell_send, cell_recv, cells, spread, turned, mixed, force,
    elev, depth, friction, mask, col_n, col_s,
    to_w, to_e, to_s, to_n, from_e, from_w, from_n, from_s,
    load_sem, send_sem, recv_sem, cell_sems, halo_send, halo_recv,
):
    steps, owned, width = values.shape
    rows, cols = out_e.shape
    slots = 2 * owned // n_lon
    total = n_lon * slots
    per_lane = 128 // slots
    n_bi, n_bj = rows // SIDE, cols // SIDE
    wide = to_s.shape[-1]
    lon, lat = lax.axis_index("lon"), lax.axis_index("lat")

    loads = [
        pltpu.make_async_copy(src, dst, load_sem.at[i])
        for i, (src, dst) in enumerate((
            (elev_in, elev.at[pl.ds(0, rows), :]), (east_in, out_u), (north_in, out_v),
            (depth_in, depth), (friction_in, friction), (mask_in, mask),
        ))
    ]
    for load in loads:
        load.start()

    barrier = pltpu.get_barrier_semaphore()

    def peer(k):
        return lax.rem(lon + k, n_lon)

    @pl.loop(1, n_lon)
    def _(k):
        pl.semaphore_signal(barrier, inc=1, device_id={"lon": peer(k)}, device_id_type=MESH)

    north_of, south_of = lax.rem(lat + 1, n_lat), lax.rem(lat + n_lat - 1, n_lat)
    for there in (north_of, south_of):
        pl.semaphore_signal(barrier, inc=1, device_id={"lat": there}, device_id_type=MESH)

    lower = hot(iota((owned, owned), 0) < iota((owned, owned), 1))
    shift = lax.rem(lon * slots, 128)

    def placed(s):
        dest = meta[s][0:1, :]
        picked = hot(iota((n_lon, owned), 0) == dest)
        before = jnp.dot(picked, lower, preferred_element_type=F32)
        place = jnp.sum(before * picked.astype(F32), axis=0, keepdims=True)
        return dest, place.astype(jnp.int32)

    bundle = jnp.zeros((n_lon * 8, 128), F32)
    for s in range(steps):
        dest, place = placed(s)
        at = iota((8, owned), 0)
        info = meta[s].astype(F32)
        line = jnp.where(at == s, info[1:2, :], jnp.where(at == steps + s, info[2:3, :], 0.0))
        line = jnp.concatenate([line] * n_lon, axis=0)
        line = jnp.where((iota((n_lon * 8, owned), 0) >> 3) == dest, line, 0.0).astype(BF16)
        lane = hot(iota((128, owned), 0) == place + shift)
        bundle = bundle + lax.dot_general(line, lane, NT, preferred_element_type=F32)
    cell_send[...] = bundle.reshape(n_lon, 8, 128)

    pl.semaphore_wait(barrier, n_lon + 1)

    @pl.loop(1, n_lon)
    def _(k):
        pltpu.make_async_remote_copy(
            src_ref=cell_send.at[peer(k)], dst_ref=cell_recv.at[lon],
            send_sem=cell_sems.at[0], recv_sem=cell_sems.at[1],
            device_id={"lon": peer(k)}, device_id_type=MESH,
        ).start()

    def post(s):
        @pl.loop(1, n_lon)
        def _(k):
            pltpu.make_async_remote_copy(
                src_ref=send.at[s, pl.ds(peer(k) * slots, slots), :],
                dst_ref=recv.at[s, pl.ds(lon * slots, slots), :],
                send_sem=send_sem.at[s], recv_sem=recv_sem.at[s],
                device_id={"lon": peer(k)}, device_id_type=MESH,
            ).start()

    @pl.loop(0, steps)
    def _(i):
        s = steps - 1 - i
        dest, place = placed(s)
        pick = hot(iota((total, owned), 0) == dest * slots + place)
        high, low = split(values[s])
        send[s] = jnp.dot(pick, high, preferred_element_type=F32) + jnp.dot(
            pick, low, preferred_element_type=F32
        )

        @pl.when(i < 2)
        def _():
            post(s)

        mine = pl.ds(pl.multiple_of(lon * slots, 8), slots)
        recv[s, mine, :] = send[s, mine, :]

    cell_recv[lon] = cell_send[lon]

    for b in range(SIDE):
        spread[b * 128:(b + 1) * 128, :] = hot(iota((128, cols), 1) == iota((128, cols), 0) * SIDE + b)
    at = iota((width, width), 0)
    turn = hot(iota((width, width), 1) == (at % SIDE) * SIDE + at // SIDE)
    eye = iota((rows, wide), 0) == iota((rows, wide), 1)

    def laid(column):
        return jnp.sum(jnp.where(eye, column, 0.0), axis=0, keepdims=True)

    def stood(line):
        return jnp.sum(jnp.where(eye, line, 0.0), axis=1, keepdims=True)

    for load in loads:
        load.wait()

    others = pl.ds(0, n_lon - 1)
    pltpu.make_async_copy(cell_recv.at[others], cell_recv.at[others], cell_sems.at[1]).wait()
    for g in range(total // 128):
        part = cell_recv[g * per_lane:(g + 1) * per_lane]
        cells[:, g * 128:(g + 1) * 128] = jnp.sum(part, axis=0)

    last = jnp.where(lat == n_lat - 1, 1, 0)
    open_lat = jnp.where(lat == 0, 0.0, 1.0)
    most = pl.ds(0, (n_lon - 1) * slots)
    end = cols - 128

    def scatter(s):
        pltpu.make_async_copy(recv.at[s, most, :], recv.at[s, most, :], recv_sem.at[s]).wait()
        bi = cells[pl.ds(s, 1), :].astype(jnp.int32)
        bj = cells[pl.ds(steps + s, 1), :].astype(jnp.int32)
        for h, part in enumerate(split(recv[s])):
            turned[h] = lax.dot_general(turn, part, NT, preferred_element_type=F32).astype(BF16)
        keep = hot((iota((rows, total), 0) // SIDE) == bi)
        column = hot(iota((128, total), 0) == bj)
        for b in range(SIDE):
            both = jnp.concatenate(
                [jnp.concatenate([turned[h, b * SIDE:(b + 1) * SIDE, :]] * n_bi, axis=0) * keep for h in range(2)],
                axis=0,
            )
            got = lax.dot_general(both, column, NT, preferred_element_type=F32)
            high, low = split(got[:rows] + got[rows:])
            mixed[:rows, b * 128:(b + 1) * 128] = high
            mixed[rows:, b * 128:(b + 1) * 128] = low
        for n in range(cols // 256):
            here = slice(n * 256, (n + 1) * 256)
            got = jnp.dot(mixed[...], spread[:, here], preferred_element_type=F32)
            force[s, :, here] = mask[:, here].astype(F32) * (got[:rows] + got[rows:])

    scatter(steps - 1)

    @pl.loop(0, steps)
    def _(i):
        s = steps - 1 - i
        elev[:rows, :] = elev[:rows, :] + force[s]
        to_w[s] = elev[0:1, :]
        to_e[s, :, 0:cols] = elev[rows - 1:rows, :]
        to_e[s, :, cols:2 * cols] = out_u[rows - 1:rows, :]
        to_e[s, :, 2 * cols:] = depth[rows - 1:rows, :] * mask[rows - 1:rows, :].astype(F32)
        first = laid(elev[:rows, 0:128][:, 0:1])
        to_s[s] = first
        to_n[s, :, 0:wide] = laid(elev[:rows, end:][:, 127:128])
        to_n[s, :, wide:2 * wide] = laid(out_v[:, end:][:, 127:128])
        to_n[s, :, 2 * wide:] = laid((depth[:, end:] * mask[:, end:].astype(F32))[:, 127:128])
        copies = [
            pltpu.make_async_remote_copy(
                src_ref=src.at[s], dst_ref=dst.at[s],
                send_sem=halo_send.at[s, q], recv_sem=halo_recv.at[s, q],
                device_id=there, device_id_type=MESH,
            )
            for q, (src, dst, there) in enumerate((
                (to_w, from_e, {"lon": peer(n_lon - 1)}),
                (to_e, from_w, {"lon": peer(1)}),
                (to_s, from_n, {"lat": south_of}),
                (to_n, from_s, {"lat": north_of}),
            ))
        ]
        for copy in copies:
            copy.start()

        @pl.when(i < steps - 2)
        def _():
            post(s - 2)

        @pl.when(i < steps - 1)
        def _():
            scatter(s - 1)

        for copy in copies:
            copy.wait()
        elev[rows:rows + 1, :] = from_e[s]
        col_n[...] = stood(from_n[s])
        side = from_s[s]
        col_s[...] = stood(
            open_lat * side[:, 2 * wide:]
            * (side[:, wide:2 * wide] + 0.25 * (first - side[:, 0:wide]))
        )
        edge = from_w[s]
        above = edge[:, 2 * cols:] * (
            edge[:, cols:2 * cols] + 0.25 * (elev[0:1, :] - edge[:, 0:cols])
        )
        row_at, lane_at = iota((8, cols), 0), iota((8, cols), 1)

        def chunk(k, above):
            here = pl.ds(pl.multiple_of(k * 8, 8), 8)
            e = elev[here, :]
            e_next = elev[pl.ds(pl.multiple_of(k * 8 + 8, 8), 8), :]
            wet = mask[here, :].astype(F32)
            wet_v = jnp.where(lane_at < cols - last, wet, 0.0)
            e_east = jnp.where(row_at == 7, e_next[0:1, :], pltpu.roll(e, 7, 0))
            e_north = jnp.where(lane_at == cols - 1, col_n[here, :], pltpu.roll(e, cols - 1, 1))
            flow_u = wet * (out_u[here, :] + 0.25 * (e_east - e))
            flow_v = wet_v * (out_v[here, :] + 0.25 * (e_north - e))
            deep = depth[here, :]
            term_u, term_v = deep * flow_u, deep * flow_v
            west = jnp.where(row_at == 0, above, pltpu.roll(term_u, 1, 0))
            south = jnp.where(lane_at == 0, col_s[here, :], pltpu.roll(term_v, 1, 1))
            e = e + 0.25 * (term_u - west) + 0.25 * (term_v - south)
            elev[here, :] = e
            out_e[here, :] = e
            slow = 1.0 - friction[here, :]
            out_u[here, :] = slow * flow_u
            out_v[here, :] = slow * flow_v
            return term_u[7:8, :]

        lax.fori_loop(0, rows // 8, chunk, above)

    pltpu.make_async_copy(cell_send.at[others], cell_send.at[others], cell_sems.at[0]).wait()

    @pl.loop(0, steps)
    def _(s):
        pltpu.make_async_copy(send.at[s, most, :], send.at[s, most, :], send_sem.at[s]).wait()


def per_device(
    n_lon, n_lat,
    adj_elev, adj_east, adj_north, depth, friction, ocean_mask, misfit_values, dest_lon, block_cell,
):
    rows, cols = adj_elev.shape
    steps, owned, width = misfit_values.shape
    slots = 2 * owned // n_lon
    total = n_lon * slots
    per_lat = cols // SIDE
    meta = jnp.stack([dest_lon[:, :, 0], block_cell // per_lat, block_cell % per_lat], axis=1)
    meta = jnp.pad(meta, ((0, 0), (0, 5), (0, 0)))
    wide = -(-rows // 128) * 128
    vmem = pl.BlockSpec(memory_space=pltpu.VMEM)
    hbm = pl.BlockSpec(memory_space=pl.ANY)
    tile = jax.ShapeDtypeStruct((rows, cols), F32)
    return pl.pallas_call(
        functools.partial(kernel, n_lon, n_lat),
        out_shape=(tile, tile, tile),
        in_specs=[vmem] * 2 + [hbm] * 6,
        out_specs=(vmem, vmem, vmem),
        scratch_shapes=[
            pltpu.VMEM((steps, total, width), F32),
            pltpu.VMEM((steps, total, width), F32),
            pltpu.VMEM((n_lon, 8, 128), F32),
            pltpu.VMEM((n_lon, 8, 128), F32),
            pltpu.VMEM((8, total), F32),
            pltpu.VMEM((SIDE * 128, cols), BF16),
            pltpu.VMEM((2, width, total), BF16),
            pltpu.VMEM((2 * rows, SIDE * 128), BF16),
            pltpu.VMEM((steps, rows, cols), F32),
            pltpu.VMEM((rows + 8, cols), F32),
            pltpu.VMEM((rows, cols), F32),
            pltpu.VMEM((rows, cols), F32),
            pltpu.VMEM((rows, cols), jnp.int32),
            pltpu.VMEM((rows, 1), F32),
            pltpu.VMEM((rows, 1), F32),
            pltpu.VMEM((steps, 1, cols), F32),
            pltpu.VMEM((steps, 1, 3 * cols), F32),
            pltpu.VMEM((steps, 1, wide), F32),
            pltpu.VMEM((steps, 1, 3 * wide), F32),
            pltpu.VMEM((steps, 1, cols), F32),
            pltpu.VMEM((steps, 1, 3 * cols), F32),
            pltpu.VMEM((steps, 1, wide), F32),
            pltpu.VMEM((steps, 1, 3 * wide), F32),
            pltpu.SemaphoreType.DMA((6,)),
            pltpu.SemaphoreType.DMA((steps,)),
            pltpu.SemaphoreType.DMA((steps,)),
            pltpu.SemaphoreType.DMA((2,)),
            pltpu.SemaphoreType.DMA((steps, 4)),
            pltpu.SemaphoreType.DMA((steps, 4)),
        ],
        compiler_params=pltpu.CompilerParams(
            collective_id=0, has_side_effects=True, vmem_limit_bytes=60 * 2**20
        ),
    )(misfit_values, meta, adj_elev, adj_east, adj_north, depth, friction, ocean_mask)


def solution(mesh):
    tile, owned = P("lon", "lat"), P(None, ("lon", "lat"))
    return jax.shard_map(
        functools.partial(per_device, mesh.shape["lon"], mesh.shape["lat"]),
        mesh=mesh,
        in_specs=(tile,) * 6 + (P(None, ("lon", "lat"), None), P(None, ("lon", "lat"), None), owned),
        out_specs=(tile, tile, tile),
        check_vma=False,
    )
```

```python
import functools

import jax
import jax.numpy as jnp
from jax import lax
from jax.experimental import pallas as pl
from jax.experimental.pallas import tpu as pltpu
from jax.sharding import PartitionSpec as P

F32, BF16 = jnp.float32, jnp.bfloat16
MESH = pl.DeviceIdType.MESH
SIDE = 16
NT = (((1,), (1,)), ((), ()))


def split(x):
    high = x.astype(BF16)
    return high, (x - high.astype(F32)).astype(BF16)


def iota(shape, dim):
    return lax.broadcasted_iota(jnp.int32, shape, dim)


def hot(condition):
    return jnp.where(condition, 1.0, 0.0).astype(BF16)


def kernel(
    n_lon, n_lat,
    values, meta, elev_in, east_in, north_in, depth_in, friction_in, mask_in,
    out_e, out_u, out_v,
    send, recv, cell_send, cell_recv, cells, spread, turned, mixed, force,
    elev, depth, friction, mask, col_n, col_s,
    to_w, to_e, to_s, to_n, from_e, from_w, from_n, from_s,
    load_sem, send_sem, recv_sem, cell_sems, halo_send, halo_recv,
):
    steps, owned, width = values.shape
    rows, cols = out_e.shape
    slots = 2 * owned // n_lon
    total = n_lon * slots
    per_lane = 128 // slots
    n_bi, n_bj = rows // SIDE, cols // SIDE
    wide = to_s.shape[-1]
    lon, lat = lax.axis_index("lon"), lax.axis_index("lat")

    loads = [
        pltpu.make_async_copy(src, dst, load_sem.at[i])
        for i, (src, dst) in enumerate((
            (elev_in, elev.at[pl.ds(0, rows), :]), (east_in, out_u), (north_in, out_v),
            (depth_in, depth), (friction_in, friction), (mask_in, mask),
        ))
    ]
    for load in loads:
        load.start()

    barrier = pltpu.get_barrier_semaphore()

    def peer(k):
        return lax.rem(lon + k, n_lon)

    @pl.loop(1, n_lon)
    def _(k):
        pl.semaphore_signal(barrier, inc=1, device_id={"lon": peer(k)}, device_id_type=MESH)

    north_of, south_of = lax.rem(lat + 1, n_lat), lax.rem(lat + n_lat - 1, n_lat)
    for there in (north_of, south_of):
        pl.semaphore_signal(barrier, inc=1, device_id={"lat": there}, device_id_type=MESH)

    lower = hot(iota((owned, owned), 0) < iota((owned, owned), 1))
    shift = lax.rem(lon * slots, 128)

    def placed(s):
        dest = meta[s][0:1, :]
        picked = hot(iota((n_lon, owned), 0) == dest)
        before = jnp.dot(picked, lower, preferred_element_type=F32)
        place = jnp.sum(before * picked.astype(F32), axis=0, keepdims=True)
        return dest, place.astype(jnp.int32)

    bundle = jnp.zeros((n_lon * 8, 128), F32)
    for s in range(steps):
        dest, place = placed(s)
        at = iota((8, owned), 0)
        info = meta[s].astype(F32)
        line = jnp.where(at == s, info[1:2, :], jnp.where(at == steps + s, info[2:3, :], 0.0))
        line = jnp.concatenate([line] * n_lon, axis=0)
        line = jnp.where((iota((n_lon * 8, owned), 0) >> 3) == dest, line, 0.0).astype(BF16)
        lane = hot(iota((128, owned), 0) == place + shift)
        bundle = bundle + lax.dot_general(line, lane, NT, preferred_element_type=F32)
    cell_send[...] = bundle.reshape(n_lon, 8, 128)

    pl.semaphore_wait(barrier, n_lon + 1)

    @pl.loop(1, n_lon)
    def _(k):
        pltpu.make_async_remote_copy(
            src_ref=cell_send.at[peer(k)], dst_ref=cell_recv.at[lon],
            send_sem=cell_sems.at[0], recv_sem=cell_sems.at[1],
            device_id={"lon": peer(k)}, device_id_type=MESH,
        ).start()

    def post(s):
        @pl.loop(1, n_lon)
        def _(k):
            pltpu.make_async_remote_copy(
                src_ref=send.at[s, pl.ds(peer(k) * slots, slots), :],
                dst_ref=recv.at[s, pl.ds(lon * slots, slots), :],
                send_sem=send_sem.at[s], recv_sem=recv_sem.at[s],
                device_id={"lon": peer(k)}, device_id_type=MESH,
            ).start()

    @pl.loop(0, steps)
    def _(i):
        s = steps - 1 - i
        dest, place = placed(s)
        pick = hot(iota((total, owned), 0) == dest * slots + place)
        high, low = split(values[s])
        send[s] = jnp.dot(pick, high, preferred_element_type=F32) + jnp.dot(
            pick, low, preferred_element_type=F32
        )

        @pl.when(i < 2)
        def _():
            post(s)

        mine = pl.ds(pl.multiple_of(lon * slots, 8), slots)
        recv[s, mine, :] = send[s, mine, :]

    cell_recv[lon] = cell_send[lon]

    for b in range(SIDE):
        spread[b * 128:(b + 1) * 128, :] = hot(iota((128, cols), 1) == iota((128, cols), 0) * SIDE + b)
    at = iota((width, width), 0)
    turn = hot(iota((width, width), 1) == (at % SIDE) * SIDE + at // SIDE)
    eye = iota((rows, wide), 0) == iota((rows, wide), 1)

    def laid(column):
        return jnp.sum(jnp.where(eye, column, 0.0), axis=0, keepdims=True)

    def stood(line):
        return jnp.sum(jnp.where(eye, line, 0.0), axis=1, keepdims=True)

    for load in loads:
        load.wait()

    others = pl.ds(0, n_lon - 1)
    pltpu.make_async_copy(cell_recv.at[others], cell_recv.at[others], cell_sems.at[1]).wait()
    for g in range(total // 128):
        part = cell_recv[g * per_lane:(g + 1) * per_lane]
        cells[:, g * 128:(g + 1) * 128] = jnp.sum(part, axis=0)

    last = jnp.where(lat == n_lat - 1, 1, 0)
    open_lat = jnp.where(lat == 0, 0.0, 1.0)
    most = pl.ds(0, (n_lon - 1) * slots)
    end = cols - 128

    def scatter(s):
        pltpu.make_async_copy(recv.at[s, most, :], recv.at[s, most, :], recv_sem.at[s]).wait()
        bi = cells[pl.ds(s, 1), :].astype(jnp.int32)
        bj = cells[pl.ds(steps + s, 1), :].astype(jnp.int32)
        for h, part in enumerate(split(recv[s])):
            turned[h] = lax.dot_general(turn, part, NT, preferred_element_type=F32).astype(BF16)
        keep = hot((iota((rows, total), 0) // SIDE) == bi)
        column = hot(iota((128, total), 0) == bj)
        for b in range(SIDE):
            both = jnp.concatenate(
                [jnp.concatenate([turned[h, b * SIDE:(b + 1) * SIDE, :]] * n_bi, axis=0) * keep for h in range(2)],
                axis=0,
            )
            got = lax.dot_general(both, column, NT, preferred_element_type=F32)
            high, low = split(got[:rows] + got[rows:])
            mixed[:rows, b * 128:(b + 1) * 128] = high
            mixed[rows:, b * 128:(b + 1) * 128] = low
        for n in range(cols // 256):
            here = slice(n * 256, (n + 1) * 256)
            got = jnp.dot(mixed[...], spread[:, here], preferred_element_type=F32)
            force[s, :, here] = mask[:, here].astype(F32) * (got[:rows] + got[rows:])

    scatter(steps - 1)

    @pl.loop(0, steps)
    def _(i):
        s = steps - 1 - i
        elev[:rows, :] = elev[:rows, :] + force[s]
        to_w[s] = elev[0:1, :]
        to_e[s, :, 0:cols] = elev[rows - 1:rows, :]
        to_e[s, :, cols:2 * cols] = out_u[rows - 1:rows, :]
        to_e[s, :, 2 * cols:] = depth[rows - 1:rows, :] * mask[rows - 1:rows, :].astype(F32)
        first = laid(elev[:rows, 0:128][:, 0:1])
        to_s[s] = first
        to_n[s, :, 0:wide] = laid(elev[:rows, end:][:, 127:128])
        to_n[s, :, wide:2 * wide] = laid(out_v[:, end:][:, 127:128])
        to_n[s, :, 2 * wide:] = laid((depth[:, end:] * mask[:, end:].astype(F32))[:, 127:128])
        copies = [
            pltpu.make_async_remote_copy(
                src_ref=src.at[s], dst_ref=dst.at[s],
                send_sem=halo_send.at[s, q], recv_sem=halo_recv.at[s, q],
                device_id=there, device_id_type=MESH,
            )
            for q, (src, dst, there) in enumerate((
                (to_w, from_e, {"lon": peer(n_lon - 1)}),
                (to_e, from_w, {"lon": peer(1)}),
                (to_s, from_n, {"lat": south_of}),
                (to_n, from_s, {"lat": north_of}),
            ))
        ]
        for copy in copies:
            copy.start()

        @pl.when(i < steps - 2)
        def _():
            post(s - 2)

        @pl.when(i < steps - 1)
        def _():
            scatter(s - 1)

        for copy in copies:
            copy.wait()
        elev[rows:rows + 1, :] = from_e[s]
        col_n[...] = stood(from_n[s])
        side = from_s[s]
        col_s[...] = stood(
            open_lat * side[:, 2 * wide:]
            * (side[:, wide:2 * wide] + 0.25 * (first - side[:, 0:wide]))
        )
        edge = from_w[s]
        above = edge[:, 2 * cols:] * (
            edge[:, cols:2 * cols] + 0.25 * (elev[0:1, :] - edge[:, 0:cols])
        )
        row_at, lane_at = iota((8, cols), 0), iota((8, cols), 1)

        def chunk(k, above):
            here = pl.ds(pl.multiple_of(k * 8, 8), 8)
            e = elev[here, :]
            e_next = elev[pl.ds(pl.multiple_of(k * 8 + 8, 8), 8), :]
            wet = mask[here, :].astype(F32)
            wet_v = jnp.where(lane_at < cols - last, wet, 0.0)
            e_east = jnp.where(row_at == 7, e_next[0:1, :], pltpu.roll(e, 7, 0))
            e_north = jnp.where(lane_at == cols - 1, col_n[here, :], pltpu.roll(e, cols - 1, 1))
            flow_u = wet * (out_u[here, :] + 0.25 * (e_east - e))
            flow_v = wet_v * (out_v[here, :] + 0.25 * (e_north - e))
            deep = depth[here, :]
            term_u, term_v = deep * flow_u, deep * flow_v
            west = jnp.where(row_at == 0, above, pltpu.roll(term_u, 1, 0))
            south = jnp.where(lane_at == 0, col_s[here, :], pltpu.roll(term_v, 1, 1))
            e = e + 0.25 * (term_u - west) + 0.25 * (term_v - south)
            elev[here, :] = e
            out_e[here, :] = e
            slow = 1.0 - friction[here, :]
            out_u[here, :] = slow * flow_u
            out_v[here, :] = slow * flow_v
            return term_u[7:8, :]

        lax.fori_loop(0, rows // 8, chunk, above, unroll=4)

    pltpu.make_async_copy(cell_send.at[others], cell_send.at[others], cell_sems.at[0]).wait()

    @pl.loop(0, steps)
    def _(s):
        pltpu.make_async_copy(send.at[s, most, :], send.at[s, most, :], send_sem.at[s]).wait()


def per_device(
    n_lon, n_lat,
    adj_elev, adj_east, adj_north, depth, friction, ocean_mask, misfit_values, dest_lon, block_cell,
):
    rows, cols = adj_elev.shape
    steps, owned, width = misfit_values.shape
    slots = 2 * owned // n_lon
    total = n_lon * slots
    per_lat = cols // SIDE
    meta = jnp.stack([dest_lon[:, :, 0], block_cell // per_lat, block_cell % per_lat], axis=1)
    meta = jnp.pad(meta, ((0, 0), (0, 5), (0, 0)))
    wide = -(-rows // 128) * 128
    vmem = pl.BlockSpec(memory_space=pltpu.VMEM)
    hbm = pl.BlockSpec(memory_space=pl.ANY)
    tile = jax.ShapeDtypeStruct((rows, cols), F32)
    return pl.pallas_call(
        functools.partial(kernel, n_lon, n_lat),
        out_shape=(tile, tile, tile),
        in_specs=[vmem] * 2 + [hbm] * 6,
        out_specs=(vmem, vmem, vmem),
        scratch_shapes=[
            pltpu.VMEM((steps, total, width), F32),
            pltpu.VMEM((steps, total, width), F32),
            pltpu.VMEM((n_lon, 8, 128), F32),
            pltpu.VMEM((n_lon, 8, 128), F32),
            pltpu.VMEM((8, total), F32),
            pltpu.VMEM((SIDE * 128, cols), BF16),
            pltpu.VMEM((2, width, total), BF16),
            pltpu.VMEM((2 * rows, SIDE * 128), BF16),
            pltpu.VMEM((steps, rows, cols), F32),
            pltpu.VMEM((rows + 8, cols), F32),
            pltpu.VMEM((rows, cols), F32),
            pltpu.VMEM((rows, cols), F32),
            pltpu.VMEM((rows, cols), jnp.int32),
            pltpu.VMEM((rows, 1), F32),
            pltpu.VMEM((rows, 1), F32),
            pltpu.VMEM((steps, 1, cols), F32),
            pltpu.VMEM((steps, 1, 3 * cols), F32),
            pltpu.VMEM((steps, 1, wide), F32),
            pltpu.VMEM((steps, 1, 3 * wide), F32),
            pltpu.VMEM((steps, 1, cols), F32),
            pltpu.VMEM((steps, 1, 3 * cols), F32),
            pltpu.VMEM((steps, 1, wide), F32),
            pltpu.VMEM((steps, 1, 3 * wide), F32),
            pltpu.SemaphoreType.DMA((6,)),
            pltpu.SemaphoreType.DMA((steps,)),
            pltpu.SemaphoreType.DMA((steps,)),
            pltpu.SemaphoreType.DMA((2,)),
            pltpu.SemaphoreType.DMA((steps, 4)),
            pltpu.SemaphoreType.DMA((steps, 4)),
        ],
        compiler_params=pltpu.CompilerParams(
            collective_id=0, has_side_effects=True, vmem_limit_bytes=60 * 2**20
        ),
    )(misfit_values, meta, adj_elev, adj_east, adj_north, depth, friction, ocean_mask)


def solution(mesh):
    tile, owned = P("lon", "lat"), P(None, ("lon", "lat"))
    return jax.shard_map(
        functools.partial(per_device, mesh.shape["lon"], mesh.shape["lat"]),
        mesh=mesh,
        in_specs=(tile,) * 6 + (P(None, ("lon", "lat"), None), P(None, ("lon", "lat"), None), owned),
        out_specs=(tile, tile, tile),
        check_vma=False,
    )
```
